256 devices in a mesh: grp: 16 (over z, core), cp: 16 (over y, x).
Axes of the slice: x: 4, y: 4, z: 8, core: 2. Of those that a mesh axis runs over, the one named last changes fastest.
Arguments:
- clean_hidden: bfloat16 [16, 2048, 5120], P('grp', 'cp'), may hold values from -6 to 6
- noisy_hidden: bfloat16 [16, 2048, 5120], P('grp', 'cp'), may hold values from -6 to 6
- noisy_query: bfloat16 [16, 2048, 1024], P('grp', 'cp'), may hold values from -288 to 288
- out_grad: bfloat16 [16, 2048, 1024], P('grp', 'cp'), may hold values from -6 to 6
- kv_weight: bfloat16 [5120, 256], replicated, may hold values from -0.078125 to 0.078125
- key_gain: float32 [128], replicated, may hold values from 0.5 to 2
- doc_lengths: int32 [16, 4], P('grp'), may hold values from 1 to 26, 32 in all within a row
- clean_place: int32 [16, 32], P('grp'), may hold values from 0 to 31, each once within a row
- noisy_place: int32 [16, 32], P('grp'), may hold values from 0 to 31, each once within a row
Outputs:
- attention_out: bfloat16 [16, 2048, 1024], P('grp', 'cp')
- query_grad: bfloat16 [16, 2048, 1024], P('grp', 'cp')
- kv_weight_grad: bfloat16 [5120, 256], P(('grp', 'cp'))
The draws below stay inside these ranges and needn't reach their ends.
Inputs may be any that keep to these rules, and one draw needn't show every extreme that they name: `doc_lengths`: each group's 4 lengths sum to 32; in every group the longest is exactly 32 - 3 * max(1, 2). `clean_place`: each group's row is a permutation of the slots. `noisy_place`: each group's row is a permutation of the slots.
All inputs are finite; a program needn't handle non-finite values.
Results may differ from the reference program's by a relative error of at most 0.033.
The reference program's roundings to bfloat16 on the way count: a program that leaves them out, or rounds other values in their place, can miss the bound.
Values may be sent and summed in bfloat16 or wider, within the bound.
No kernel may reach another device: no remote copies, remote signals or barrier semaphores. Data moves between devices by JAX's collectives and lax.ppermute only.
A program may use at most 128 MiB of HBM per device.

```python
import math
import jax
import jax.numpy as jnp
import numpy as np
from jax import lax

D = 5120
HD = 128
H = 8
BLK = 64
DOCS = 4
GROUPS = 16
GROUP_TOKENS = 2048
BLOCKS = 32


def draw_noisy_query(key, part):
    key = jax.random.fold_in(key, 11)
    first_key = jax.random.fold_in(key, 0)
    samples = jnp.clip(jax.random.normal(first_key, (GROUPS, GROUP_TOKENS, H * HD), jnp.float32), -6.0, 6.0)
    return samples.astype(jnp.bfloat16)


def spiked(values, key, source, target, blocks, factor):
    def block_of(axis_at):
        return (jnp.arange(values.shape[axis_at]) // (values.shape[axis_at] // blocks)).reshape((-1,) + (1,) * (values.ndim - 1 - axis_at))

    first = jax.random.permutation(key, blocks)[block_of(target)]
    far = (block_of(target) + blocks // 2) % blocks
    return jnp.where((block_of(source) == first) | (block_of(source) == far), factor * values, values)


def block_scale(own_key, dims, pieces, low, top_value):
    gain = 1.0
    for axis_at, blocks in pieces:
        heights = jax.random.uniform(jax.random.fold_in(jax.random.fold_in(own_key, 6), axis_at), (blocks,), jnp.float32, low / len(pieces), top_value / len(pieces))
        gain = gain * jnp.repeat(jnp.exp(heights), dims[axis_at] // blocks).reshape((-1,) + (1,) * (len(dims) - 1 - axis_at))
    return gain


def profile(number_of, total, reach, slope):
    loads = [(1 << 20) // math.isqrt(standing ** slope) + 1 for standing in range(2, number_of + 1)]
    surplus, counts = total - reach - (number_of - 1), [1] * (number_of - 1)
    while surplus > 0:
        free = [i for i in range(number_of - 1) if counts[i] < reach]
        mass, left = sum([loads[i] for i in free]), surplus
        for i in free:
            addition = min(reach - counts[i], max(1, left * loads[i] // mass), surplus)
            counts[i] = counts[i] + addition
            surplus = surplus - addition
    return np.array([reach] + counts)


def uneven(key, count, total, limit, slope):
    if count == 2:
        one = jax.random.randint(key, (), max(1, total - limit), min(limit, total - 1) + 1)
        return jnp.stack([one, total - one])
    sizes = jnp.asarray(profile(count, total, limit, slope), jnp.int32)
    twos = (count - 1) // 2
    donor, sink = sizes[1:1 + 2 * twos:2], sizes[2:2 + 2 * twos:2]
    slack = jnp.minimum(donor - 1, limit - sink)
    moved = jax.random.randint(jax.random.fold_in(key, 1), (twos,), 0, 1 << 20) % (slack + 1)
    sizes = sizes.at[1:1 + 2 * twos:2].set(donor - moved).at[2:2 + 2 * twos:2].set(sink + moved)
    return sizes[jax.random.permutation(jax.random.fold_in(key, 2), count)]


def noise(rng, extent, scale, most, shards=(), kind=jnp.bfloat16):
    values = jax.random.normal(rng, extent, jnp.float32) * scale
    if len(shards) > 0:
        values = block_scale(rng, extent, shards, -0.22, 0.18) * values
    return jnp.clip(values, min=-most, max=most).astype(kind)


def noise_with(key, shape, deviation, bound, cuts, heavy, held_as=jnp.bfloat16):
    result = deviation * jax.random.normal(key, shape, jnp.float32)
    if cuts:
        result = result * block_scale(key, shape, cuts, -0.22, 0.18)
    return jnp.clip(spiked(result, jax.random.fold_in(key, 3), *heavy), -bound, bound).astype(held_as)


def setup_inputs(seed: int = 0) -> dict:
    splits = jax.random.split(jax.random.key(seed), 10)
    clean_hidden = noise_with(splits[0], (GROUPS, GROUP_TOKENS, D), 1.0, 6.0, ((0, 16), (1, 16)), (1, 2, 16, 2.0))
    noisy_hidden = noise_with(splits[1], (GROUPS, GROUP_TOKENS, D), 1.0, 6.0, ((0, 16), (1, 16)), (1, 2, 16, 2.0))
    noisy_query = draw_noisy_query(jax.random.fold_in(splits[9], 71), 0)
    out_grad = noise(splits[3], (GROUPS, GROUP_TOKENS, H * HD), 1.0, 6.0, ((0, 16), (1, 16)))
    kv_weight = noise(splits[4], (D, 2 * HD), D ** -0.5, 0.078125)
    key_gain = jnp.clip(jnp.exp(jax.random.uniform(splits[5], (HD,), jnp.float32, math.log(0.5), math.log(2.0))), 0.5, 2.0)
    doc_lengths = jax.vmap(lambda own: uneven(own, DOCS, BLOCKS, BLOCKS - (DOCS - 1) * max(1, BLOCKS // 16), 2))(jax.random.split(splits[6], GROUPS)).reshape((GROUPS, DOCS)).astype(jnp.int32)
    clean_place = jax.vmap(lambda own: jax.random.permutation(own, BLOCKS))(jax.random.split(splits[7], GROUPS)).reshape((GROUPS, BLOCKS)).astype(jnp.int32)
    noisy_place = jax.vmap(lambda own: jax.random.permutation(own, BLOCKS))(jax.random.split(splits[8], GROUPS)).reshape((GROUPS, BLOCKS)).astype(jnp.int32)
    return dict(clean_hidden=clean_hidden, noisy_hidden=noisy_hidden, noisy_query=noisy_query, out_grad=out_grad, kv_weight=kv_weight, key_gain=key_gain, doc_lengths=doc_lengths, clean_place=clean_place, noisy_place=noisy_place)


EPSILON = 1e-06
NEGATIVE = -1e+30

def lowered(values):
    return lax.optimization_barrier(values.astype(jnp.bfloat16)).astype(jnp.float32)

def project_rows(hidden_rows, kv_weight, key_gain):
    joined = jnp.dot(hidden_rows, kv_weight, preferred_element_type=jnp.float32)
    pre_key = joined[:, :HD]
    inverse = lax.rsqrt(lax.optimization_barrier(jnp.mean(pre_key * pre_key, axis=1, keepdims=True)) + EPSILON)
    key_rows = (pre_key * inverse * key_gain).astype(jnp.bfloat16)
    value_rows = joined[:, HD:].astype(jnp.bfloat16)
    return (key_rows, value_rows, pre_key, inverse)

def norm_back(key_grads, pre_key, inverse, key_gain):
    scaled = key_grads * key_gain
    inner_sum = lax.optimization_barrier(jnp.mean(scaled * pre_key, axis=1, keepdims=True))
    return inverse * scaled - pre_key * inverse * inverse * inverse * inner_sum

def reference(clean_hidden, noisy_hidden, noisy_query, out_grad, kv_weight, key_gain, doc_lengths, clean_place, noisy_place):
    scaling = HD ** (-0.5)

    def one_group(carried, group_items):
        clean_rows, noisy_rows, query_all, grad_all, lengths, c_place, n_place = group_items
        keys_c, values_c, pre_c, inv_c = project_rows(clean_rows, kv_weight, key_gain)
        keys_n, values_n, pre_n, inv_n = project_rows(noisy_rows, kv_weight, key_gain)
        blocks = jnp.arange(BLOCKS, dtype=jnp.int32)
        clean_order = jnp.zeros((BLOCKS,), jnp.int32).at[c_place].set(blocks)
        noisy_order = jnp.zeros((BLOCKS,), jnp.int32).at[n_place].set(blocks)
        doc_ends = jnp.cumsum(lengths).astype(jnp.int32)
        doc_of = lax.optimization_barrier(jnp.sum((doc_ends[None, :] <= blocks[:, None]).astype(jnp.int32), axis=1))
        key_log = jnp.repeat(clean_order, BLK)
        key_doc = doc_of[key_log]
        clean_keys = keys_c.astype(jnp.float32)
        clean_values = values_c.astype(jnp.float32)
        own_key_all = keys_n.astype(jnp.float32).reshape(BLOCKS, BLK, HD)
        own_value_all = values_n.astype(jnp.float32).reshape(BLOCKS, BLK, HD)
        queries = query_all.astype(jnp.float32).reshape(BLOCKS, BLK, H, HD)
        grads = grad_all.astype(jnp.float32).reshape(BLOCKS, BLK, H, HD)

        def one_block(summed, position):
            query_log = noisy_order[position]
            query_doc = doc_of[query_log]
            allowed = (key_doc == query_doc) & (key_log < query_log)
            query_rows = queries[position]
            grad_rows = grads[position]
            own_keys = own_key_all[position]
            own_values = own_value_all[position]
            clean_s = jnp.where(allowed[None, None, :], jnp.einsum('rhd,kd->hrk', query_rows, clean_keys) * scaling, NEGATIVE)
            self_s = jnp.einsum('rhd,kd->hrk', query_rows, own_keys) * scaling
            row_max = jnp.maximum(lax.optimization_barrier(jnp.max(clean_s, axis=2)), lax.optimization_barrier(jnp.max(self_s, axis=2)))
            sum_exp = lax.optimization_barrier(jnp.sum(jnp.exp(clean_s - row_max[:, :, None]), axis=2)) + lax.optimization_barrier(jnp.sum(jnp.exp(self_s - row_max[:, :, None]), axis=2))
            log_total = (row_max + jnp.log(sum_exp))[:, :, None]
            clean_p = jnp.exp(clean_s - log_total)
            self_p = jnp.exp(self_s - log_total)
            clean_low = lowered(clean_p)
            self_low = lowered(self_p)
            block_out = (jnp.einsum('hrk,kd->rhd', clean_low, clean_values) + jnp.einsum('hrk,kd->rhd', self_low, own_values)).astype(jnp.bfloat16)
            row_delta = lax.optimization_barrier(jnp.sum(grad_rows * block_out.astype(jnp.float32), axis=2)).T[:, :, None]
            clean_ds = lowered(clean_p * (jnp.einsum('rhd,kd->hrk', grad_rows, clean_values) - row_delta))
            self_ds = lowered(self_p * (jnp.einsum('rhd,kd->hrk', grad_rows, own_values) - row_delta))
            block_qgrad = jnp.einsum('hrk,kd->rhd', clean_ds, clean_keys) * scaling + jnp.einsum('hrk,kd->rhd', self_ds, own_keys) * scaling
            clean_part = jnp.concatenate([jnp.einsum('hrk,rhd->kd', clean_ds, query_rows) * scaling, jnp.einsum('hrk,rhd->kd', clean_low, grad_rows)], axis=1)
            self_part = jnp.concatenate([jnp.einsum('hrk,rhd->kd', self_ds, query_rows) * scaling, jnp.einsum('hrk,rhd->kd', self_low, grad_rows)], axis=1)
            return (summed + clean_part, (block_out.reshape(BLK, H * HD), block_qgrad.astype(jnp.bfloat16).reshape(BLK, H * HD), self_part))
        clean_total, (outputs, query_grads, noisy_total) = lax.scan(one_block, jnp.zeros((GROUP_TOKENS, 2 * HD), jnp.float32), blocks)
        noisy_total = noisy_total.reshape(GROUP_TOKENS, 2 * HD)
        clean_grad = jnp.concatenate([norm_back(clean_total[:, :HD], pre_c, inv_c, key_gain), clean_total[:, HD:]], axis=1).astype(jnp.bfloat16)
        noisy_grad = jnp.concatenate([norm_back(noisy_total[:, :HD], pre_n, inv_n, key_gain), noisy_total[:, HD:]], axis=1).astype(jnp.bfloat16)
        weight_term = jnp.dot(clean_rows.T, clean_grad, preferred_element_type=jnp.float32) + jnp.dot(noisy_rows.T, noisy_grad, preferred_element_type=jnp.float32)
        return (carried + weight_term, (outputs.reshape(GROUP_TOKENS, H * HD), query_grads.reshape(GROUP_TOKENS, H * HD)))
    weight_total, (attention_out, query_grad) = lax.scan(one_group, jnp.zeros((D, 2 * HD), jnp.float32), (clean_hidden, noisy_hidden, noisy_query, out_grad, doc_lengths, clean_place, noisy_place))
    return (attention_out, query_grad, weight_total.astype(jnp.bfloat16))
```

```python
import functools

import jax
import jax.numpy as jnp
from jax import lax
from jax.experimental import pallas as pl
from jax.experimental.pallas import tpu as pltpu
from jax.sharding import Mesh
from jax.sharding import PartitionSpec as P

BLK = 64
EPSILON = 1e-06
NEGATIVE = -1e30
VMEM_LIMIT = 56 * 1024 * 1024

F32 = jnp.float32
BF16 = jnp.bfloat16


def project_kernel(
    cp_ref, len_ref, cplace_ref, nplace_ref, clean_ref, noisy_ref, w_ref, gain_ref,
    spread_ref, nkv_ref, pre_ref, bias_ref, acc_ref,
):
    step = pl.program_id(0)
    rows, hd = clean_ref.shape[0], gain_ref.shape[1]
    hidden = jnp.concatenate([clean_ref[...], noisy_ref[...]], axis=0)
    part = jnp.dot(hidden, w_ref[...], preferred_element_type=F32)

    @pl.when(step == 0)
    def _():
        acc_ref[...] = part
        blocks, docs = cplace_ref.shape[1], len_ref.shape[1]
        keys = blocks * BLK
        logical, starts = [], []
        for local in range(rows // BLK):
            slot = cp_ref[0, 0] * (rows // BLK) + local
            log = jnp.int32(0)
            for b in range(blocks):
                log = log + jnp.where(nplace_ref[0, b] == slot, b, 0)
            end, start = jnp.int32(0), jnp.int32(0)
            for d in range(docs):
                end = end + len_ref[0, d]
                start = jnp.where(end <= log, end, start)
            logical.append(log)
            starts.append(start)
        row = lax.broadcasted_iota(jnp.int32, (8, keys), 0)
        slots = lax.broadcasted_iota(jnp.int32, (8, keys), 1) // BLK
        key_log = jnp.zeros((8, keys), jnp.int32)
        for b in range(blocks):
            key_log = jnp.where(slots == cplace_ref[0, b], b, key_log)
        low = jnp.where(row == 0, starts[0], starts[1])
        high = jnp.where(row == 0, logical[0], logical[1])
        bias_ref[:, :keys] = jnp.where((key_log >= low) & (key_log < high), 0.0, NEGATIVE)
        own = lax.broadcasted_iota(jnp.int32, (8, rows), 1) // BLK
        bias_ref[:, keys:] = jnp.where(
            own == lax.broadcasted_iota(jnp.int32, (8, rows), 0), 0.0, NEGATIVE
        )

    @pl.when(step > 0)
    def _():
        acc_ref[...] += part

    @pl.when(step == pl.num_programs(0) - 1)
    def _():
        pre = acc_ref[:, :hd]
        inverse = lax.rsqrt(jnp.mean(pre * pre, axis=1, keepdims=True) + EPSILON)
        keys = (pre * inverse * gain_ref[...]).astype(BF16)
        values = acc_ref[:, hd:].astype(BF16)
        pre_ref[...] = pre
        nkv_ref[:, :hd] = keys[rows:]
        nkv_ref[:, hd:] = values[rows:]
        for dest in range(spread_ref.shape[0]):
            spread_ref[dest, :, :hd] = keys[:rows]
            spread_ref[dest, :, hd:] = values[:rows]


def attention_kernel(
    q_ref, do_ref, ckv_ref, nkv_ref, bias_ref,
    out_ref, dq_ref, dkv_ref, dnkv_ref,
    k_ref, v_ref, mask_ref, qs_ref, dos_ref, p_ref, ds_ref,
):
    tok, heads = q_ref.shape[0], q_ref.shape[1] // 128
    hd = 128
    scale = hd ** (-0.5)
    peers = ckv_ref.shape[0]
    for c in range(peers):
        k_ref[c * tok : (c + 1) * tok, :] = ckv_ref[c, :, :hd]
        v_ref[c * tok : (c + 1) * tok, :] = ckv_ref[c, :, hd:]
    k_ref[peers * tok :, :] = nkv_ref[:, :hd]
    v_ref[peers * tok :, :] = nkv_ref[:, hd:]
    total = k_ref.shape[0]
    for local in range(tok // BLK):
        mask_ref[local * BLK : (local + 1) * BLK, :] = jnp.broadcast_to(
            bias_ref[local : local + 1, :], (BLK, total)
        )
    for h in range(heads):
        qs_ref[h * tok : (h + 1) * tok, :] = q_ref[:, h * hd : (h + 1) * hd]
        dos_ref[h * tok : (h + 1) * tok, :] = do_ref[:, h * hd : (h + 1) * hd]

    def one_head(h, carry):
        at = pl.ds(pl.multiple_of(h * tok, tok), tok)
        cols = pl.ds(pl.multiple_of(h * hd, hd), hd)
        q, do = qs_ref[at, :], dos_ref[at, :]
        s = lax.dot_general(q, k_ref[...], (((1,), (1,)), ((), ())), preferred_element_type=F32)
        s = s * scale + mask_ref[...]
        e = jnp.exp(s - jnp.max(s, axis=1, keepdims=True))
        p = e * (1.0 / jnp.sum(e, axis=1, keepdims=True))
        p_low = p.astype(BF16)
        p_ref[at, :] = p_low
        out = jnp.dot(p_low, v_ref[...], preferred_element_type=F32).astype(BF16)
        out_ref[:, cols] = out
        delta = jnp.sum(do.astype(F32) * out.astype(F32), axis=1, keepdims=True)
        dp = lax.dot_general(do, v_ref[...], (((1,), (1,)), ((), ())), preferred_element_type=F32)
        ds = (p * (dp - delta)).astype(BF16)
        ds_ref[at, :] = ds
        dq = jnp.dot(ds, k_ref[...], preferred_element_type=F32) * scale
        dq_ref[:, cols] = dq.astype(BF16)
        return carry

    lax.fori_loop(0, heads, one_head, 0)
    q_t = qs_ref[...].T
    do_t = dos_ref[...].T

    def one_peer(c, carry):
        cols = pl.ds(pl.multiple_of(c * tok, tok), tok)
        dk = jnp.dot(q_t, ds_ref[:, cols], preferred_element_type=F32) * scale
        dv = jnp.dot(do_t, p_ref[:, cols], preferred_element_type=F32)
        dkv_ref[c, :hd, :] = dk.astype(BF16)
        dkv_ref[c, hd:, :] = dv.astype(BF16)
        return carry

    lax.fori_loop(0, peers, one_peer, 0)
    dnkv_ref[:hd, :] = jnp.dot(q_t, ds_ref[:, peers * tok :], preferred_element_type=F32) * scale
    dnkv_ref[hd:, :] = jnp.dot(do_t, p_ref[:, peers * tok :], preferred_element_type=F32)


def weight_kernel(
    core_ref, recv_ref, dnkv_ref, pre_ref, gain_ref, clean_ref, noisy_ref,
    send_ref, keep_ref, g_ref, dw_ref,
):
    step = pl.program_id(0)
    rows, hd = clean_ref.shape[0], gain_ref.shape[1]
    width = clean_ref.shape[1]
    half = width // 2
    peers, per = send_ref.shape[0], send_ref.shape[1]

    @pl.when(step == 0)
    def _():
        summed = recv_ref[0].astype(F32)
        for c in range(1, recv_ref.shape[0]):
            summed = summed + recv_ref[c].astype(F32)
        for copy, grad_t in enumerate((summed, dnkv_ref[...])):
            at = slice(copy * rows, (copy + 1) * rows)
            pre = pre_ref[at, :]
            inverse = lax.rsqrt(jnp.mean(pre * pre, axis=1, keepdims=True) + EPSILON)
            scaled = grad_t[:hd].T * gain_ref[...]
            inner = jnp.mean(scaled * pre, axis=1, keepdims=True)
            pre_grad = inverse * scaled - pre * inverse * inverse * inverse * inner
            g_ref[at, :hd] = pre_grad.astype(BF16)
            g_ref[at, hd:] = grad_t[hd:].T.astype(BF16)

    hidden = jnp.concatenate([clean_ref[...], noisy_ref[...]], axis=0)
    term = lax.dot_general(
        hidden, g_ref[...], (((0,), (0,)), ((), ())), preferred_element_type=F32
    )
    at = pl.ds(pl.multiple_of(step * half, half), half)
    for core in range(2):
        for lane in range(2):
            dw_ref[core, lane, at, :] = term[
                core * half : (core + 1) * half, lane * 128 : (lane + 1) * 128
            ]

    @pl.when(step == pl.num_programs(0) - 1)
    def _():
        mine = core_ref[0, 0]
        zs = pl.num_programs(0)

        def one_peer(j, carry):
            for ref, core in ((send_ref, 1 - mine), (keep_ref, mine)):
                for i in range(per):
                    for lane in range(2):
                        piece = dw_ref[core, lane, pl.ds(j * per + i, 8, stride=half), :]
                        ref[j, i, :, lane * 128 : (lane + 1) * 128] = piece.astype(BF16)
            return carry

        lax.fori_loop(0, peers, one_peer, 0)


def per_device(
    clean_hidden, noisy_hidden, noisy_query, out_grad, kv_weight, key_gain,
    doc_lengths, clean_place, noisy_place,
):
    rows, width = clean_hidden.shape[1:]
    hd = key_gain.shape[0]
    peers = lax.axis_size(("y", "x"))
    zs = lax.axis_size("z")
    blocks = clean_place.shape[1]
    keys = blocks * BLK
    total = keys + rows
    heads = noisy_query.shape[2] // hd
    clean, noisy = clean_hidden[0], noisy_hidden[0]
    gain = key_gain.reshape(1, hd)
    cp_index = lax.axis_index(("y", "x")).reshape(1, 1).astype(jnp.int32)
    core_index = lax.axis_index("core").reshape(1, 1).astype(jnp.int32)
    smem = pl.BlockSpec(memory_space=pltpu.SMEM)
    params = pltpu.CompilerParams(vmem_limit_bytes=VMEM_LIMIT)

    def whole(*shape):
        return pl.BlockSpec(shape, lambda *_: (0,) * len(shape))

    steps = 5
    part = width // steps
    spread, nkv, pre, bias = pl.pallas_call(
        project_kernel,
        grid=(steps,),
        in_specs=[smem, smem, smem, smem]
        + [pl.BlockSpec((rows, part), lambda s: (0, s))] * 2
        + [pl.BlockSpec((part, 2 * hd), lambda s: (s, 0)), whole(1, hd)],
        out_specs=[
            whole(peers, rows, 2 * hd),
            whole(rows, 2 * hd),
            whole(2 * rows, hd),
            whole(8, total),
        ],
        out_shape=[
            jax.ShapeDtypeStruct((peers, rows, 2 * hd), BF16),
            jax.ShapeDtypeStruct((rows, 2 * hd), BF16),
            jax.ShapeDtypeStruct((2 * rows, hd), F32),
            jax.ShapeDtypeStruct((8, total), F32),
        ],
        scratch_shapes=[pltpu.VMEM((2 * rows, 2 * hd), F32)],
        compiler_params=params,
        name="project",
    )(cp_index, doc_lengths, clean_place, noisy_place, clean, noisy, kv_weight, gain)

    gathered = lax.all_to_all(spread, ("y", "x"), 0, 0, tiled=True)

    attention, query_grad, dkv, dnkv = pl.pallas_call(
        attention_kernel,
        out_shape=[
            jax.ShapeDtypeStruct((rows, heads * hd), BF16),
            jax.ShapeDtypeStruct((rows, heads * hd), BF16),
            jax.ShapeDtypeStruct((peers, 2 * hd, rows), BF16),
            jax.ShapeDtypeStruct((2 * hd, rows), F32),
        ],
        scratch_shapes=[
            pltpu.VMEM((total, hd), BF16),
            pltpu.VMEM((total, hd), BF16),
            pltpu.VMEM((rows, total), F32),
            pltpu.VMEM((heads * rows, hd), BF16),
            pltpu.VMEM((heads * rows, hd), BF16),
            pltpu.VMEM((heads * rows, total), BF16),
            pltpu.VMEM((heads * rows, total), BF16),
        ],
        compiler_params=params,
        name="attend",
    )(noisy_query[0], out_grad[0], gathered, nkv, bias)

    received = lax.all_to_all(dkv, ("y", "x"), 0, 0, tiled=True)

    slab = width // zs
    per = slab // (2 * peers)
    piece = jax.ShapeDtypeStruct((peers, per, zs, 2 * hd), BF16)
    send, keep = pl.pallas_call(
        weight_kernel,
        grid=(zs,),
        in_specs=[
            smem,
            whole(peers, 2 * hd, rows),
            whole(2 * hd, rows),
            whole(2 * rows, hd),
            whole(1, hd),
        ]
        + [pl.BlockSpec((rows, slab), lambda s: (0, s))] * 2,
        out_specs=[whole(peers, per, zs, 2 * hd)] * 2,
        out_shape=[piece, piece],
        scratch_shapes=[
            pltpu.VMEM((2 * rows, 2 * hd), BF16),
            pltpu.VMEM((2, 2, zs * slab // 2, 128), F32),
        ],
        compiler_params=params,
        name="weight",
    )(core_index, received, dnkv, pre, gain, clean, noisy)

    other = lax.ppermute(send, "core", [(0, 1), (1, 0)])
    both = (keep.astype(F32) + other.astype(F32)).astype(BF16)
    both = lax.all_to_all(both, ("y", "x"), 0, 0, tiled=True)
    term = jnp.sum(both.astype(F32), axis=0).astype(BF16)
    term = lax.all_to_all(jnp.swapaxes(term, 0, 1), "z", 0, 0, tiled=True)
    share = jnp.sum(term.astype(F32), axis=0).astype(BF16)
    return (attention[None], query_grad[None], share)


def solution(mesh):
    zs, cps = mesh.devices.shape[0] // 2, mesh.devices.shape[1]
    side = int(round(cps**0.5))
    grid = Mesh(mesh.devices.reshape(zs, 2, cps // side, side), ("z", "core", "y", "x"))
    grp, cp = ("z", "core"), ("y", "x")
    in_specs = (
        P(grp, cp, None),
        P(grp, cp, None),
        P(grp, cp, None),
        P(grp, cp, None),
        P(),
        P(),
        P(grp, None),
        P(grp, None),
        P(grp, None),
    )
    out_specs = (P(grp, cp, None), P(grp, cp, None), P(grp + cp, None))
    return jax.shard_map(
        per_device, mesh=grid, in_specs=in_specs, out_specs=out_specs, check_vma=False
    )
```

```python
import jax
import jax.numpy as jnp
from jax import lax
from jax.experimental import pallas as pl
from jax.experimental.pallas import tpu as pltpu
from jax.sharding import Mesh
from jax.sharding import PartitionSpec as P

BLK = 64
EPSILON = 1e-06
NEGATIVE = -1e30
MIB = 1024 * 1024
LOG2E = 1.4426950408889634

F32 = jnp.float32
BF16 = jnp.bfloat16


def keys_values(joined, gain):
    hd = gain.shape[1]
    pre = joined[:, :hd]
    inverse = lax.rsqrt(jnp.mean(pre * pre, axis=1, keepdims=True) + EPSILON)
    return pre, (pre * inverse * gain).astype(BF16), joined[:, hd:].astype(BF16)


def accumulate(acc_ref, part):
    step = pl.program_id(0)

    @pl.when(step == 0)
    def _():
        acc_ref[...] = part

    @pl.when(step > 0)
    def _():
        acc_ref[...] += part


def clean_kernel(clean_ref, w_ref, gain_ref, spread_ref, pre_ref, acc_ref):
    hd = gain_ref.shape[1]
    accumulate(acc_ref, jnp.dot(clean_ref[...], w_ref[...], preferred_element_type=F32))

    @pl.when(pl.program_id(0) == pl.num_programs(0) - 1)
    def _():
        pre, keys, values = keys_values(acc_ref[...], gain_ref[...])
        pre_ref[...] = pre
        for dest in range(spread_ref.shape[0]):
            spread_ref[dest, :, :hd] = keys
            spread_ref[dest, :, hd:] = values


def prepare_kernel(
    cp_ref, core_ref, len_ref, cplace_ref, nplace_ref, clean_ref, noisy_ref, w_ref, gain_ref,
    nkv_ref, pre_ref, mask_ref, mine_ref, other_ref, acc_ref, turned_ref,
):
    step = pl.program_id(0)
    rows, hd = noisy_ref.shape[0], gain_ref.shape[1]
    half = noisy_ref.shape[1] // 2
    peers, per = mine_ref.shape[0], mine_ref.shape[1]
    accumulate(acc_ref, jnp.dot(noisy_ref[...], w_ref[...], preferred_element_type=F32))
    turned = jnp.concatenate([clean_ref[...], noisy_ref[...]], axis=0).T.astype(F32)
    at = pl.ds(pl.multiple_of(step * half, half), half)
    for core in range(2):
        for lane in range(2):
            turned_ref[core, lane, at, :] = turned[
                core * half : (core + 1) * half, lane * 128 : (lane + 1) * 128
            ]

    @pl.when(step == 0)
    def _():
        blocks, docs = cplace_ref.shape[1], len_ref.shape[1]
        locals_ = rows // BLK
        logical, starts = [], []
        for local in range(locals_):
            slot = cp_ref[0, 0] * locals_ + local
            log = jnp.int32(0)
            for b in range(blocks):
                log = log + jnp.where(nplace_ref[0, b] == slot, b, 0)
            end, start = jnp.int32(0), jnp.int32(0)
            for d in range(docs):
                end = end + len_ref[0, d]
                start = jnp.where(end <= log, end, start)
            logical.append(log)
            starts.append(start)
        lane = lax.broadcasted_iota(jnp.int32, (BLK, hd), 1)
        for b in range(blocks):
            tile = jnp.zeros((BLK, hd), F32)
            for local in range(locals_):
                hidden = jnp.where((starts[local] <= b) & (b < logical[local]), 0.0, NEGATIVE)
                tile = jnp.where(lane == local, hidden, tile)
            slot = pl.multiple_of(cplace_ref[0, b] * BLK, BLK)
            mask_ref[pl.ds(slot, BLK), :] = tile.astype(BF16)
        for local in range(locals_):
            tile = jnp.where((lane < locals_) & (lane != local), NEGATIVE, 0.0)
            first = blocks * BLK + local * BLK
            mask_ref[first : first + BLK, :] = tile.astype(BF16)

    @pl.when(step == pl.num_programs(0) - 1)
    def _():
        pre, keys, values = keys_values(acc_ref[...], gain_ref[...])
        pre_ref[...] = pre
        nkv_ref[:, :hd] = keys
        nkv_ref[:, hd:] = values
        core = core_ref[0, 0]

        def one_peer(j, carry):
            for ref, side in ((other_ref, 1 - core), (mine_ref, core)):
                for i in range(per):
                    for lane in range(2):
                        piece = turned_ref[side, lane, pl.ds(j * per + i, 8, stride=half), :]
                        ref[j, i, :, lane * 128 : (lane + 1) * 128] = piece.astype(BF16)
            return carry

        lax.fori_loop(0, peers, one_peer, 0)


def attention_kernel(
    q_ref, do_ref, ckv_ref, nkv_ref, mask_ref,
    out_ref, dq_ref, dkv_ref, dnkv_ref,
    kx_ref, vx_ref, qx_ref, dox_ref, e_ref, p_ref, ds_ref,
):
    hd = 128
    tok, heads = q_ref.shape[0], q_ref.shape[1] // hd
    scale = hd ** (-0.5)
    peers = ckv_ref.shape[0]
    total = kx_ref.shape[0]
    for c in range(peers):
        kx_ref[c * tok : (c + 1) * tok, :hd] = ckv_ref[c, :, :hd]
        vx_ref[c * tok : (c + 1) * tok, :hd] = ckv_ref[c, :, hd:]
    kx_ref[peers * tok :, :hd] = nkv_ref[:, :hd]
    vx_ref[peers * tok :, :hd] = nkv_ref[:, hd:]
    kx_ref[:, hd:] = mask_ref[...]
    vx_ref[:, hd:] = jnp.ones((total, hd), BF16)
    lane = lax.broadcasted_iota(jnp.int32, (tok, hd), 1)
    block = lax.broadcasted_iota(jnp.int32, (tok, hd), 0) // BLK
    pick = jnp.where(lane == block, 1.0, 0.0).astype(BF16)
    for h in range(heads):
        at = slice(h * tok, (h + 1) * tok)
        qx_ref[at, :hd] = q_ref[:, h * hd : (h + 1) * hd]
        qx_ref[at, hd:] = pick

    def transposed(a, b):
        return lax.dot_general(a, b, (((1,), (1,)), ((), ())), preferred_element_type=F32)

    group = 2 * tok

    def weigh(g, carry):
        at = pl.ds(pl.multiple_of(g * group, group), group)
        s = transposed(qx_ref[at, :], kx_ref[...])
        e = jnp.exp2((s - jnp.max(s, axis=1, keepdims=True)) * (scale * LOG2E))
        e_ref[at, :] = e
        p_ref[at, :] = e.astype(BF16)
        return carry

    lax.fori_loop(0, heads * tok // group, weigh, 0)
    for h in range(heads):
        at, cols = slice(h * tok, (h + 1) * tok), slice(h * hd, (h + 1) * hd)
        o = jnp.dot(p_ref[at, :], vx_ref[...], preferred_element_type=F32)
        over = 1.0 / o[:, hd:]
        out = (o[:, :hd] * over).astype(BF16)
        out_ref[:, cols] = out
        do = (do_ref[:, cols].astype(F32) * over).astype(BF16)
        delta = jnp.sum(do.astype(F32) * out.astype(F32), axis=1, keepdims=True)
        high = delta.astype(BF16).astype(F32)
        middle = (delta - high).astype(BF16).astype(F32)
        low = delta - high - middle
        parts = jnp.where(lane == 0, -high, jnp.where(lane == 1, -middle, -low))
        dox_ref[at, :hd] = do
        dox_ref[at, hd:] = jnp.where(lane < 3, parts, 0.0).astype(BF16)

    def slope(g, carry):
        at = pl.ds(pl.multiple_of(g * group, group), group)
        dp = transposed(dox_ref[at, :], vx_ref[...])
        ds_ref[at, :] = (e_ref[at, :] * dp).astype(BF16)
        return carry

    lax.fori_loop(0, heads * tok // group, slope, 0)
    for h in range(heads):
        at, cols = slice(h * tok, (h + 1) * tok), slice(h * hd, (h + 1) * hd)
        dq = jnp.dot(ds_ref[at, :], kx_ref[:, :hd], preferred_element_type=F32)
        dq_ref[:, cols] = (dq * scale).astype(BF16)
    q_t = qx_ref[:, :hd].T
    do_t = dox_ref[:, :hd].T
    wide = 4

    def one_peer(c, carry):
        cols = pl.ds(pl.multiple_of(c * wide * tok, wide * tok), wide * tok)
        dk = jnp.dot(q_t, ds_ref[:, cols], preferred_element_type=F32) * scale
        dv = jnp.dot(do_t, p_ref[:, cols], preferred_element_type=F32)
        for i in range(wide):
            dkv_ref[c * wide + i, :hd, :] = dk[:, i * tok : (i + 1) * tok].astype(BF16)
            dkv_ref[c * wide + i, hd:, :] = dv[:, i * tok : (i + 1) * tok].astype(BF16)
        return carry

    lax.fori_loop(0, peers // wide, one_peer, 0)
    dnkv_ref[:hd, :] = jnp.dot(q_t, ds_ref[:, peers * tok :], preferred_element_type=F32) * scale
    dnkv_ref[hd:, :] = jnp.dot(do_t, p_ref[:, peers * tok :], preferred_element_type=F32)


def row_grad_kernel(recv_ref, dnkv_ref, cpre_ref, npre_ref, gain_ref, g_ref):
    rows, hd = cpre_ref.shape
    summed = recv_ref[0].astype(F32)
    for c in range(1, recv_ref.shape[0]):
        summed = summed + recv_ref[c].astype(F32)
    for copy, (grad_t, pre_ref) in enumerate(((summed, cpre_ref), (dnkv_ref[...], npre_ref))):
        at = slice(copy * rows, (copy + 1) * rows)
        pre = pre_ref[...]
        inverse = lax.rsqrt(jnp.mean(pre * pre, axis=1, keepdims=True) + EPSILON)
        scaled = grad_t[:hd].T * gain_ref[...]
        inner = jnp.mean(scaled * pre, axis=1, keepdims=True)
        pre_grad = inverse * scaled - pre * inverse * inverse * inverse * inner
        g_ref[at, :hd] = pre_grad.astype(BF16)
        g_ref[at, hd:] = grad_t[hd:].T.astype(BF16)


def weight_kernel(mine_ref, theirs_ref, g_ref, their_g_ref, dw_ref):
    dw_ref[...] = (
        jnp.dot(mine_ref[...], g_ref[...], preferred_element_type=F32)
        + jnp.dot(theirs_ref[...], their_g_ref[...], preferred_element_type=F32)
    ).astype(BF16)


def whole(*shape):
    return pl.BlockSpec(shape, lambda *_: (0,) * len(shape))


def limit(mib):
    return pltpu.CompilerParams(vmem_limit_bytes=mib * MIB)


def per_device(
    clean_hidden, noisy_hidden, noisy_query, out_grad, kv_weight, key_gain,
    doc_lengths, clean_place, noisy_place,
):
    rows, width = clean_hidden.shape[1:]
    hd = key_gain.shape[0]
    cp = ("y", "x")
    peers, zs = lax.axis_size(cp), lax.axis_size("z")
    total = clean_place.shape[1] * BLK + rows
    heads = noisy_query.shape[2] // hd
    clean, noisy = clean_hidden[0], noisy_hidden[0]
    gain = key_gain.reshape(1, hd)
    cp_index = lax.axis_index(cp).reshape(1, 1).astype(jnp.int32)
    core_index = lax.axis_index("core").reshape(1, 1).astype(jnp.int32)
    smem = pl.BlockSpec(memory_space=pltpu.SMEM)
    shape = jax.ShapeDtypeStruct
    swap = [(0, 1), (1, 0)]

    steps = 5
    part = width // steps
    spread, clean_pre = pl.pallas_call(
        clean_kernel,
        grid=(steps,),
        in_specs=[
            pl.BlockSpec((rows, part), lambda s: (0, s)),
            pl.BlockSpec((part, 2 * hd), lambda s: (s, 0)),
            whole(1, hd),
        ],
        out_specs=[whole(peers, rows, 2 * hd), whole(rows, hd)],
        out_shape=[shape((peers, rows, 2 * hd), BF16), shape((rows, hd), F32)],
        scratch_shapes=[pltpu.VMEM((rows, 2 * hd), F32)],
        compiler_params=limit(10),
        cost_estimate=pl.CostEstimate(
            flops=4 * rows * width * hd, bytes_accessed=5 * MIB, transcendentals=0
        ),
        name="clean",
    )(clean, kv_weight, gain)

    spread, clean_later, noisy_later = lax.optimization_barrier((spread, clean, noisy))
    gathered = lax.all_to_all(spread, cp, 0, 0, tiled=True)

    slab = width // zs
    per = slab // (2 * peers)
    turned = shape((peers, per, zs, 2 * rows), BF16)
    nkv, noisy_pre, mask, mine, other = pl.pallas_call(
        prepare_kernel,
        grid=(zs,),
        in_specs=[smem] * 5
        + [pl.BlockSpec((rows, slab), lambda s: (0, s))] * 2
        + [pl.BlockSpec((slab, 2 * hd), lambda s: (s, 0)), whole(1, hd)],
        out_specs=[
            whole(rows, 2 * hd),
            whole(rows, hd),
            whole(total, hd),
            whole(*turned.shape),
            whole(*turned.shape),
        ],
        out_shape=[
            shape((rows, 2 * hd), BF16),
            shape((rows, hd), F32),
            shape((total, hd), BF16),
            turned,
            turned,
        ],
        scratch_shapes=[
            pltpu.VMEM((rows, 2 * hd), F32),
            pltpu.VMEM((2, 2, width // 2, 128), F32),
        ],
        compiler_params=limit(24),
        cost_estimate=pl.CostEstimate(
            flops=4 * rows * width * hd, bytes_accessed=12 * MIB, transcendentals=0
        ),
        name="prepare",
    )(
        cp_index, core_index, doc_lengths, clean_place, noisy_place,
        clean_later, noisy_later, kv_weight, gain,
    )
    theirs = lax.ppermute(other, "core", swap)

    attention, query_grad, dkv, dnkv = pl.pallas_call(
        attention_kernel,
        out_shape=[
            shape((rows, heads * hd), BF16),
            shape((rows, heads * hd), BF16),
            shape((peers, 2 * hd, rows), BF16),
            shape((2 * hd, rows), F32),
        ],
        scratch_shapes=[
            pltpu.VMEM((total, 2 * hd), BF16),
            pltpu.VMEM((total, 2 * hd), BF16),
            pltpu.VMEM((heads * rows, 2 * hd), BF16),
            pltpu.VMEM((heads * rows, 2 * hd), BF16),
            pltpu.VMEM((heads * rows, total), F32),
            pltpu.VMEM((heads * rows, total), BF16),
            pltpu.VMEM((heads * rows, total), BF16),
        ],
        compiler_params=limit(44),
        cost_estimate=pl.CostEstimate(
            flops=12 * heads * rows * total * hd,
            bytes_accessed=4 * MIB,
            transcendentals=heads * rows * total,
        ),
        name="attend",
    )(noisy_query[0], out_grad[0], gathered, nkv, mask)

    received = lax.all_to_all(dkv, cp, 0, 0, tiled=True)

    row_grad = pl.pallas_call(
        row_grad_kernel,
        out_shape=shape((2 * rows, 2 * hd), BF16),
        compiler_params=limit(8),
        name="row_grad",
    )(received, dnkv, clean_pre, noisy_pre, gain)
    their_grad = lax.ppermute(row_grad, "core", swap)

    columns = width // 2
    tile = columns // 4
    flat = (columns, 2 * rows)
    both = pl.pallas_call(
        weight_kernel,
        grid=(columns // tile,),
        in_specs=[pl.BlockSpec((tile, 2 * rows), lambda s: (s, 0))] * 2
        + [whole(2 * rows, 2 * hd)] * 2,
        out_specs=pl.BlockSpec((tile, 2 * hd), lambda s: (s, 0)),
        out_shape=shape((columns, 2 * hd), BF16),
        compiler_params=limit(8),
        name="weight",
    )(mine.reshape(flat), theirs.reshape(flat), row_grad, their_grad)

    both = lax.all_to_all(both.reshape(peers, per, zs, 2 * hd), cp, 0, 0, tiled=True)
    term = jnp.sum(both.astype(F32), axis=0).astype(BF16)
    term = lax.all_to_all(jnp.swapaxes(term, 0, 1), "z", 0, 0, tiled=True)
    share = jnp.sum(term.astype(F32), axis=0).astype(BF16)
    return (attention[None], query_grad[None], share)


def solution(mesh):
    zs, cps = mesh.devices.shape[0] // 2, mesh.devices.shape[1]
    side = int(round(cps**0.5))
    grid = Mesh(mesh.devices.reshape(zs, 2, cps // side, side), ("z", "core", "y", "x"))
    grp, cp = ("z", "core"), ("y", "x")
    in_specs = (
        P(grp, cp, None),
        P(grp, cp, None),
        P(grp, cp, None),
        P(grp, cp, None),
        P(),
        P(),
        P(grp, None),
        P(grp, None),
        P(grp, None),
    )
    out_specs = (P(grp, cp, None), P(grp, cp, None), P(grp + cp, None))
    return jax.shard_map(
        per_device, mesh=grid, in_specs=in_specs, out_specs=out_specs, check_vma=False
    )
```

```python
import jax
import jax.numpy as jnp
from jax import lax
from jax.experimental import pallas as pl
from jax.experimental.pallas import tpu as pltpu
from jax.sharding import Mesh
from jax.sharding import PartitionSpec as P

BLK = 64
EPSILON = 1e-06
NEGATIVE = -1e30
MIB = 1024 * 1024
LOG2E = 1.4426950408889634

F32 = jnp.float32
BF16 = jnp.bfloat16


def keys_values(joined, gain):
    hd = gain.shape[1]
    pre = joined[:, :hd]
    inverse = lax.rsqrt(jnp.mean(pre * pre, axis=1, keepdims=True) + EPSILON)
    return pre, (pre * inverse * gain).astype(BF16), joined[:, hd:].astype(BF16)


def accumulate(acc_ref, part):
    step = pl.program_id(0)

    @pl.when(step == 0)
    def _():
        acc_ref[...] = part

    @pl.when(step > 0)
    def _():
        acc_ref[...] += part


def clean_kernel(
    clean_ref, w_ref, gain_ref, spread_ref, pre_ref,
    rows_ref, weight_ref, kv_ref, rows_sem, weight_sem, out_sem,
):
    hd = gain_ref.shape[1]
    parts = rows_ref.shape[0]
    part = rows_ref.shape[2]
    loads = []
    for i in range(parts):
        at = pl.ds(i * part, part)
        loads.append(
            (
                pltpu.make_async_copy(w_ref.at[at, :], weight_ref.at[i], weight_sem.at[i]),
                pltpu.make_async_copy(clean_ref.at[:, at], rows_ref.at[i], rows_sem.at[i]),
            )
        )
        for load in loads[i]:
            load.start()
    joined = None
    for i in range(parts):
        for load in loads[i]:
            load.wait()
        term = jnp.dot(rows_ref[i], weight_ref[i], preferred_element_type=F32)
        joined = term if joined is None else joined + term
    pre, keys, values = keys_values(joined, gain_ref[...])
    pre_ref[...] = pre
    kv_ref[:, :hd] = keys
    kv_ref[:, hd:] = values
    stores = [
        pltpu.make_async_copy(kv_ref, spread_ref.at[dest], out_sem.at[dest])
        for dest in range(spread_ref.shape[0])
    ]
    for store in stores:
        store.start()
    for store in stores:
        store.wait()


def prepare_kernel(
    cp_ref, core_ref, len_ref, cplace_ref, nplace_ref, clean_ref, noisy_ref, w_ref, gain_ref,
    nkv_ref, pre_ref, mask_ref, mine_ref, other_ref, acc_ref, turned_ref,
):
    step = pl.program_id(0)
    rows, hd = noisy_ref.shape[0], gain_ref.shape[1]
    half = noisy_ref.shape[1] // 2
    peers, per = mine_ref.shape[0], mine_ref.shape[1]
    accumulate(acc_ref, jnp.dot(noisy_ref[...], w_ref[...], preferred_element_type=F32))
    turned = jnp.concatenate([clean_ref[...], noisy_ref[...]], axis=0).T.astype(F32)
    at = pl.ds(pl.multiple_of(step * half, half), half)
    for core in range(2):
        for lane in range(2):
            turned_ref[core, lane, at, :] = turned[
                core * half : (core + 1) * half, lane * 128 : (lane + 1) * 128
            ]

    @pl.when(step == 0)
    def _():
        blocks, docs = cplace_ref.shape[1], len_ref.shape[1]
        locals_ = rows // BLK
        logical, starts = [], []
        for local in range(locals_):
            slot = cp_ref[0, 0] * locals_ + local
            log = jnp.int32(0)
            for b in range(blocks):
                log = log + jnp.where(nplace_ref[0, b] == slot, b, 0)
            end, start = jnp.int32(0), jnp.int32(0)
            for d in range(docs):
                end = end + len_ref[0, d]
                start = jnp.where(end <= log, end, start)
            logical.append(log)
            starts.append(start)
        lane = lax.broadcasted_iota(jnp.int32, (BLK, hd), 1)
        for b in range(blocks):
            tile = jnp.zeros((BLK, hd), F32)
            for local in range(locals_):
                hidden = jnp.where((starts[local] <= b) & (b < logical[local]), 0.0, NEGATIVE)
                tile = jnp.where(lane == local, hidden, tile)
            slot = pl.multiple_of(cplace_ref[0, b] * BLK, BLK)
            mask_ref[pl.ds(slot, BLK), :] = tile.astype(BF16)
        for local in range(locals_):
            tile = jnp.where((lane < locals_) & (lane != local), NEGATIVE, 0.0)
            first = blocks * BLK + local * BLK
            mask_ref[first : first + BLK, :] = tile.astype(BF16)

    @pl.when(step == pl.num_programs(0) - 1)
    def _():
        pre, keys, values = keys_values(acc_ref[...], gain_ref[...])
        pre_ref[...] = pre
        nkv_ref[:, :hd] = keys
        nkv_ref[:, hd:] = values
        core = core_ref[0, 0]

        def one_peer(j, carry):
            for ref, side in ((other_ref, 1 - core), (mine_ref, core)):
                for i in range(per):
                    for lane in range(2):
                        piece = turned_ref[side, lane, pl.ds(j * per + i, 8, stride=half), :]
                        ref[j, i, :, lane * 128 : (lane + 1) * 128] = piece.astype(BF16)
            return carry

        lax.fori_loop(0, peers, one_peer, 0)


def attention_kernel(
    q_ref, do_ref, ckv_ref, nkv_ref, mask_ref,
    out_ref, dq_ref, dkv_ref, dnkv_ref,
    kx_ref, vx_ref, qx_ref, dox_ref, e_ref, p_ref, ds_ref,
):
    hd = 128
    tok, heads = q_ref.shape[0], q_ref.shape[1] // hd
    scale = hd ** (-0.5)
    peers = ckv_ref.shape[0]
    total = kx_ref.shape[0]
    for c in range(peers):
        kx_ref[c * tok : (c + 1) * tok, :hd] = ckv_ref[c, :, :hd]
        vx_ref[c * tok : (c + 1) * tok, :hd] = ckv_ref[c, :, hd:]
    kx_ref[peers * tok :, :hd] = nkv_ref[:, :hd]
    vx_ref[peers * tok :, :hd] = nkv_ref[:, hd:]
    kx_ref[:, hd:] = mask_ref[...]
    vx_ref[:, hd:] = jnp.ones((total, hd), BF16)
    lane = lax.broadcasted_iota(jnp.int32, (tok, hd), 1)
    block = lax.broadcasted_iota(jnp.int32, (tok, hd), 0) // BLK
    pick = jnp.where(lane == block, 1.0, 0.0).astype(BF16)
    for h in range(heads):
        at = slice(h * tok, (h + 1) * tok)
        qx_ref[at, :hd] = q_ref[:, h * hd : (h + 1) * hd]
        qx_ref[at, hd:] = pick

    def transposed(a, b):
        return lax.dot_general(a, b, (((1,), (1,)), ((), ())), preferred_element_type=F32)

    group = 2 * tok

    def weigh(g, carry):
        at = pl.ds(pl.multiple_of(g * group, group), group)
        s = transposed(qx_ref[at, :], kx_ref[...])
        e = jnp.exp2((s - jnp.max(s, axis=1, keepdims=True)) * (scale * LOG2E))
        e_ref[at, :] = e
        p_ref[at, :] = e.astype(BF16)
        return carry

    lax.fori_loop(0, heads * tok // group, weigh, 0, unroll=True)
    for h in range(heads):
        at, cols = slice(h * tok, (h + 1) * tok), slice(h * hd, (h + 1) * hd)
        o = jnp.dot(p_ref[at, :], vx_ref[...], preferred_element_type=F32)
        over = 1.0 / o[:, hd:]
        out = (o[:, :hd] * over).astype(BF16)
        out_ref[:, cols] = out
        do = (do_ref[:, cols].astype(F32) * over).astype(BF16)
        delta = jnp.sum(do.astype(F32) * out.astype(F32), axis=1, keepdims=True)
        high = delta.astype(BF16).astype(F32)
        middle = (delta - high).astype(BF16).astype(F32)
        low = delta - high - middle
        parts = jnp.where(lane == 0, -high, jnp.where(lane == 1, -middle, -low))
        dox_ref[at, :hd] = do
        dox_ref[at, hd:] = jnp.where(lane < 3, parts, 0.0).astype(BF16)

    def slope(g, carry):
        at = pl.ds(pl.multiple_of(g * group, group), group)
        dp = transposed(dox_ref[at, :], vx_ref[...])
        ds_ref[at, :] = (e_ref[at, :] * dp).astype(BF16)
        return carry

    lax.fori_loop(0, heads * tok // group, slope, 0, unroll=True)
    for h in range(heads):
        at, cols = slice(h * tok, (h + 1) * tok), slice(h * hd, (h + 1) * hd)
        dq = jnp.dot(ds_ref[at, :], kx_ref[:, :hd], preferred_element_type=F32)
        dq_ref[:, cols] = (dq * scale).astype(BF16)
    q_t = qx_ref[:, :hd].T
    do_t = dox_ref[:, :hd].T
    wide = 4

    def one_peer(c, carry):
        cols = pl.ds(pl.multiple_of(c * wide * tok, wide * tok), wide * tok)
        dk = jnp.dot(q_t, ds_ref[:, cols], preferred_element_type=F32) * scale
        dv = jnp.dot(do_t, p_ref[:, cols], preferred_element_type=F32)
        for i in range(wide):
            dkv_ref[c * wide + i, :hd, :] = dk[:, i * tok : (i + 1) * tok].astype(BF16)
            dkv_ref[c * wide + i, hd:, :] = dv[:, i * tok : (i + 1) * tok].astype(BF16)
        return carry

    lax.fori_loop(0, peers // wide, one_peer, 0, unroll=True)
    dnkv_ref[:hd, :] = jnp.dot(q_t, ds_ref[:, peers * tok :], preferred_element_type=F32) * scale
    dnkv_ref[hd:, :] = jnp.dot(do_t, p_ref[:, peers * tok :], preferred_element_type=F32)


def row_grad_kernel(recv_ref, dnkv_ref, cpre_ref, npre_ref, gain_ref, g_ref):
    rows, hd = cpre_ref.shape
    summed = recv_ref[0].astype(F32)
    for c in range(1, recv_ref.shape[0]):
        summed = summed + recv_ref[c].astype(F32)
    for copy, (grad_t, pre_ref) in enumerate(((summed, cpre_ref), (dnkv_ref[...], npre_ref))):
        at = slice(copy * rows, (copy + 1) * rows)
        pre = pre_ref[...]
        inverse = lax.rsqrt(jnp.mean(pre * pre, axis=1, keepdims=True) + EPSILON)
        scaled = grad_t[:hd].T * gain_ref[...]
        inner = jnp.mean(scaled * pre, axis=1, keepdims=True)
        pre_grad = inverse * scaled - pre * inverse * inverse * inverse * inner
        g_ref[at, :hd] = pre_grad.astype(BF16)
        g_ref[at, hd:] = grad_t[hd:].T.astype(BF16)


def weight_kernel(mine_ref, theirs_ref, g_ref, their_g_ref, dw_ref):
    dw_ref[...] = (
        jnp.dot(mine_ref[...], g_ref[...], preferred_element_type=F32)
        + jnp.dot(theirs_ref[...], their_g_ref[...], preferred_element_type=F32)
    ).astype(BF16)


def whole(*shape):
    return pl.BlockSpec(shape, lambda *_: (0,) * len(shape))


def limit(mib):
    return pltpu.CompilerParams(vmem_limit_bytes=mib * MIB)


def per_device(
    clean_hidden, noisy_hidden, noisy_query, out_grad, kv_weight, key_gain,
    doc_lengths, clean_place, noisy_place,
):
    rows, width = clean_hidden.shape[1:]
    hd = key_gain.shape[0]
    cp = ("y", "x")
    peers, zs = lax.axis_size(cp), lax.axis_size("z")
    total = clean_place.shape[1] * BLK + rows
    heads = noisy_query.shape[2] // hd
    clean, noisy = clean_hidden[0], noisy_hidden[0]
    gain = key_gain.reshape(1, hd)
    cp_index = lax.axis_index(cp).reshape(1, 1).astype(jnp.int32)
    core_index = lax.axis_index("core").reshape(1, 1).astype(jnp.int32)
    smem = pl.BlockSpec(memory_space=pltpu.SMEM)
    shape = jax.ShapeDtypeStruct
    swap = [(0, 1), (1, 0)]

    parts = 5
    part = width // parts
    anywhere = pl.BlockSpec(memory_space=pl.ANY)
    spread, clean_pre = pl.pallas_call(
        clean_kernel,
        in_specs=[anywhere, anywhere, pl.BlockSpec(memory_space=pltpu.VMEM)],
        out_specs=[anywhere, pl.BlockSpec(memory_space=pltpu.VMEM)],
        out_shape=[shape((peers, rows, 2 * hd), BF16), shape((rows, hd), F32)],
        scratch_shapes=[
            pltpu.VMEM((parts, rows, part), BF16),
            pltpu.VMEM((parts, part, 2 * hd), BF16),
            pltpu.VMEM((rows, 2 * hd), BF16),
            pltpu.SemaphoreType.DMA((parts,)),
            pltpu.SemaphoreType.DMA((parts,)),
            pltpu.SemaphoreType.DMA((peers,)),
        ],
        compiler_params=limit(60),
        cost_estimate=pl.CostEstimate(
            flops=4 * rows * width * hd, bytes_accessed=5 * MIB, transcendentals=0
        ),
        name="clean",
    )(clean, kv_weight, gain)

    spread, clean_later, noisy_later = lax.optimization_barrier((spread, clean, noisy))
    gathered = lax.all_to_all(spread, cp, 0, 0, tiled=True)

    slab = width // zs
    per = slab // (2 * peers)
    turned = shape((peers, per, zs, 2 * rows), BF16)
    nkv, noisy_pre, mask, mine, other = pl.pallas_call(
        prepare_kernel,
        grid=(zs,),
        in_specs=[smem] * 5
        + [pl.BlockSpec((rows, slab), lambda s: (0, s))] * 2
        + [pl.BlockSpec((slab, 2 * hd), lambda s: (s, 0)), whole(1, hd)],
        out_specs=[
            whole(rows, 2 * hd),
            whole(rows, hd),
            whole(total, hd),
            whole(*turned.shape),
            whole(*turned.shape),
        ],
        out_shape=[
            shape((rows, 2 * hd), BF16),
            shape((rows, hd), F32),
            shape((total, hd), BF16),
            turned,
            turned,
        ],
        scratch_shapes=[
            pltpu.VMEM((rows, 2 * hd), F32),
            pltpu.VMEM((2, 2, width // 2, 128), F32),
        ],
        compiler_params=limit(63),
        cost_estimate=pl.CostEstimate(
            flops=4 * rows * width * hd, bytes_accessed=12 * MIB, transcendentals=0
        ),
        name="prepare",
    )(
        cp_index, core_index, doc_lengths, clean_place, noisy_place,
        clean_later, noisy_later, kv_weight, gain,
    )
    theirs = lax.ppermute(other, "core", swap)

    attention, query_grad, dkv, dnkv = pl.pallas_call(
        attention_kernel,
        out_shape=[
            shape((rows, heads * hd), BF16),
            shape((rows, heads * hd), BF16),
            shape((peers, 2 * hd, rows), BF16),
            shape((2 * hd, rows), F32),
        ],
        scratch_shapes=[
            pltpu.VMEM((total, 2 * hd), BF16),
            pltpu.VMEM((total, 2 * hd), BF16),
            pltpu.VMEM((heads * rows, 2 * hd), BF16),
            pltpu.VMEM((heads * rows, 2 * hd), BF16),
            pltpu.VMEM((heads * rows, total), F32),
            pltpu.VMEM((heads * rows, total), BF16),
            pltpu.VMEM((heads * rows, total), BF16),
        ],
        compiler_params=limit(60),
        cost_estimate=pl.CostEstimate(
            flops=12 * heads * rows * total * hd,
            bytes_accessed=4 * MIB,
            transcendentals=heads * rows * total,
        ),
        name="attend",
    )(noisy_query[0], out_grad[0], gathered, nkv, mask)

    received = lax.all_to_all(dkv, cp, 0, 0, tiled=True)

    row_grad = pl.pallas_call(
        row_grad_kernel,
        out_shape=shape((2 * rows, 2 * hd), BF16),
        compiler_params=limit(8),
        name="row_grad",
    )(received, dnkv, clean_pre, noisy_pre, gain)
    their_grad = lax.ppermute(row_grad, "core", swap)

    columns = width // 2
    tile = columns // 4
    flat = (columns, 2 * rows)
    both = pl.pallas_call(
        weight_kernel,
        grid=(columns // tile,),
        in_specs=[pl.BlockSpec((tile, 2 * rows), lambda s: (s, 0))] * 2
        + [whole(2 * rows, 2 * hd)] * 2,
        out_specs=pl.BlockSpec((tile, 2 * hd), lambda s: (s, 0)),
        out_shape=shape((columns, 2 * hd), BF16),
        compiler_params=limit(8),
        name="weight",
    )(mine.reshape(flat), theirs.reshape(flat), row_grad, their_grad)

    both = lax.all_to_all(both.reshape(peers, per, zs, 2 * hd), cp, 0, 0, tiled=True)
    term = jnp.sum(both.astype(F32), axis=0).astype(BF16)
    term = lax.all_to_all(jnp.swapaxes(term, 0, 1), "z", 0, 0, tiled=True)
    share = jnp.sum(term.astype(F32), axis=0).astype(BF16)
    return (attention[None], query_grad[None], share)


def solution(mesh):
    zs, cps = mesh.devices.shape[0] // 2, mesh.devices.shape[1]
    side = int(round(cps**0.5))
    grid = Mesh(mesh.devices.reshape(zs, 2, cps // side, side), ("z", "core", "y", "x"))
    grp, cp = ("z", "core"), ("y", "x")
    in_specs = (
        P(grp, cp, None),
        P(grp, cp, None),
        P(grp, cp, None),
        P(grp, cp, None),
        P(),
        P(),
        P(grp, None),
        P(grp, None),
        P(grp, None),
    )
    out_specs = (P(grp, cp, None), P(grp, cp, None), P(grp + cp, None))
    return jax.shard_map(
        per_device, mesh=grid, in_specs=in_specs, out_specs=out_specs, check_vma=False
    )
```

```python
import jax
import jax.numpy as jnp
from jax import lax
from jax.experimental import pallas as pl
from jax.experimental.pallas import tpu as pltpu
from jax.sharding import Mesh
from jax.sharding import PartitionSpec as P

BLK = 64
EPSILON = 1e-06
NEGATIVE = -1e30
MIB = 1024 * 1024
LOG2E = 1.4426950408889634

F32 = jnp.float32
BF16 = jnp.bfloat16


def keys_values(joined, gain):
    hd = gain.shape[1]
    pre = joined[:, :hd]
    inverse = lax.rsqrt(jnp.mean(pre * pre, axis=1, keepdims=True) + EPSILON)
    return pre, (pre * inverse * gain).astype(BF16), joined[:, hd:].astype(BF16)


def accumulate(acc_ref, part):
    step = pl.program_id(0)

    @pl.when(step == 0)
    def _():
        acc_ref[...] = part

    @pl.when(step > 0)
    def _():
        acc_ref[...] += part


def clean_kernel(
    clean_ref, w_ref, gain_ref, spread_ref, pre_ref,
    rows_ref, weight_ref, kv_ref, rows_sem, weight_sem, out_sem,
):
    hd = gain_ref.shape[1]
    parts = rows_ref.shape[0]
    part = rows_ref.shape[2]
    loads = []
    for i in range(parts):
        at = pl.ds(i * part, part)
        loads.append(
            (
                pltpu.make_async_copy(w_ref.at[at, :], weight_ref.at[i], weight_sem.at[i]),
                pltpu.make_async_copy(clean_ref.at[:, at], rows_ref.at[i], rows_sem.at[i]),
            )
        )
        for load in loads[i]:
            load.start()
    joined = None
    for i in range(parts):
        for load in loads[i]:
            load.wait()
        term = jnp.dot(rows_ref[i], weight_ref[i], preferred_element_type=F32)
        joined = term if joined is None else joined + term
    pre, keys, values = keys_values(joined, gain_ref[...])
    pre_ref[...] = pre
    kv_ref[:, :hd] = keys
    kv_ref[:, hd:] = values
    stores = [
        pltpu.make_async_copy(kv_ref, spread_ref.at[dest], out_sem.at[dest])
        for dest in range(spread_ref.shape[0])
    ]
    for store in stores:
        store.start()
    for store in stores:
        store.wait()


def prepare_kernel(
    cp_ref, core_ref, len_ref, cplace_ref, nplace_ref, clean_ref, noisy_ref, w_ref, gain_ref,
    nkv_ref, pre_ref, mask_ref, mine_ref, other_ref, acc_ref, turned_ref,
):
    step = pl.program_id(0)
    rows, hd = noisy_ref.shape[0], gain_ref.shape[1]
    half = noisy_ref.shape[1] // 2
    peers, per = mine_ref.shape[0], mine_ref.shape[1]
    accumulate(acc_ref, jnp.dot(noisy_ref[...], w_ref[...], preferred_element_type=F32))
    turned = jnp.concatenate([clean_ref[...], noisy_ref[...]], axis=0).T.astype(F32)
    at = pl.ds(pl.multiple_of(step * half, half), half)
    for core in range(2):
        for lane in range(2):
            turned_ref[core, lane, at, :] = turned[
                core * half : (core + 1) * half, lane * 128 : (lane + 1) * 128
            ]

    @pl.when(step == 0)
    def _():
        blocks, docs = cplace_ref.shape[1], len_ref.shape[1]
        locals_ = rows // BLK
        logical, starts = [], []
        for local in range(locals_):
            slot = cp_ref[0, 0] * locals_ + local
            log = jnp.int32(0)
            for b in range(blocks):
                log = log + jnp.where(nplace_ref[0, b] == slot, b, 0)
            end, start = jnp.int32(0), jnp.int32(0)
            for d in range(docs):
                end = end + len_ref[0, d]
                start = jnp.where(end <= log, end, start)
            logical.append(log)
            starts.append(start)
        lane = lax.broadcasted_iota(jnp.int32, (BLK, hd), 1)
        for b in range(blocks):
            tile = jnp.zeros((BLK, hd), F32)
            for local in range(locals_):
                hidden = jnp.where((starts[local] <= b) & (b < logical[local]), 0.0, NEGATIVE)
                tile = jnp.where(lane == local, hidden, tile)
            slot = pl.multiple_of(cplace_ref[0, b] * BLK, BLK)
            mask_ref[pl.ds(slot, BLK), :] = tile.astype(BF16)
        for local in range(locals_):
            tile = jnp.where((lane < locals_) & (lane != local), NEGATIVE, 0.0)
            first = blocks * BLK + local * BLK
            mask_ref[first : first + BLK, :] = tile.astype(BF16)

    @pl.when(step == pl.num_programs(0) - 1)
    def _():
        pre, keys, values = keys_values(acc_ref[...], gain_ref[...])
        pre_ref[...] = pre
        nkv_ref[:, :hd] = keys
        nkv_ref[:, hd:] = values
        core = core_ref[0, 0]

        def one_peer(j, carry):
            for ref, side in ((other_ref, 1 - core), (mine_ref, core)):
                for i in range(per):
                    for lane in range(2):
                        piece = turned_ref[side, lane, pl.ds(j * per + i, 8, stride=half), :]
                        ref[j, i, :, lane * 128 : (lane + 1) * 128] = piece.astype(BF16)
            return carry

        lax.fori_loop(0, peers, one_peer, 0)


def attention_kernel(
    q_ref, do_ref, ckv_ref, nkv_ref, mask_ref,
    out_ref, dq_ref, dkv_ref, dnkv_ref,
    kx_ref, vx_ref, qx_ref, dox_ref, p_ref, ds_ref,
):
    hd = 128
    tok, heads = q_ref.shape[0], q_ref.shape[1] // hd
    scale = hd ** (-0.5)
    peers = ckv_ref.shape[0]
    total = kx_ref.shape[0]
    for c in range(peers):
        kx_ref[c * tok : (c + 1) * tok, :hd] = ckv_ref[c, :, :hd]
        vx_ref[c * tok : (c + 1) * tok, :hd] = ckv_ref[c, :, hd:]
    kx_ref[peers * tok :, :hd] = nkv_ref[:, :hd]
    vx_ref[peers * tok :, :hd] = nkv_ref[:, hd:]
    kx_ref[:, hd:] = mask_ref[...]
    vx_ref[:, hd:] = jnp.ones((total, hd), BF16)
    lane = lax.broadcasted_iota(jnp.int32, (tok, hd), 1)
    block = lax.broadcasted_iota(jnp.int32, (tok, hd), 0) // BLK
    pick = jnp.where(lane == block, 1.0, 0.0).astype(BF16)
    for h in range(heads):
        at = slice(h * tok, (h + 1) * tok)
        qx_ref[at, :hd] = q_ref[:, h * hd : (h + 1) * hd]
        qx_ref[at, hd:] = pick

    def transposed(a, b):
        return lax.dot_general(a, b, (((1,), (1,)), ((), ())), preferred_element_type=F32)

    group = 2 * tok

    def weigh(g, carry):
        at = pl.ds(pl.multiple_of(g * group, group), group)
        s = transposed(qx_ref[at, :], kx_ref[...])
        e = jnp.exp2((s - jnp.max(s, axis=1, keepdims=True)) * (scale * LOG2E))
        p_ref[at, :] = e.astype(BF16)
        return carry

    lax.fori_loop(0, heads * tok // group, weigh, 0, unroll=True)
    for h in range(heads):
        at, cols = slice(h * tok, (h + 1) * tok), slice(h * hd, (h + 1) * hd)
        o = jnp.dot(p_ref[at, :], vx_ref[...], preferred_element_type=F32)
        over = 1.0 / o[:, hd:]
        out = (o[:, :hd] * over).astype(BF16)
        out_ref[:, cols] = out
        do = (do_ref[:, cols].astype(F32) * over).astype(BF16)
        delta = jnp.sum(do.astype(F32) * out.astype(F32), axis=1, keepdims=True)
        high = delta.astype(BF16).astype(F32)
        middle = (delta - high).astype(BF16).astype(F32)
        low = delta - high - middle
        parts = jnp.where(lane == 0, -high, jnp.where(lane == 1, -middle, -low))
        dox_ref[at, :hd] = do
        dox_ref[at, hd:] = jnp.where(lane < 3, parts, 0.0).astype(BF16)

    def slope(g, carry):
        at = pl.ds(pl.multiple_of(g * group, group), group)
        dp = transposed(dox_ref[at, :], vx_ref[...])
        ds_ref[at, :] = (p_ref[at, :].astype(F32) * dp).astype(BF16)
        return carry

    lax.fori_loop(0, heads * tok // group, slope, 0, unroll=True)
    for h in range(heads):
        at, cols = slice(h * tok, (h + 1) * tok), slice(h * hd, (h + 1) * hd)
        dq = jnp.dot(ds_ref[at, :], kx_ref[:, :hd], preferred_element_type=F32)
        dq_ref[:, cols] = (dq * scale).astype(BF16)
    q_t = qx_ref[:, :hd].T
    do_t = dox_ref[:, :hd].T
    wide = 4

    def one_peer(c, carry):
        cols = pl.ds(pl.multiple_of(c * wide * tok, wide * tok), wide * tok)
        dk = jnp.dot(q_t, ds_ref[:, cols], preferred_element_type=F32) * scale
        dv = jnp.dot(do_t, p_ref[:, cols], preferred_element_type=F32)
        for i in range(wide):
            dkv_ref[c * wide + i, :hd, :] = dk[:, i * tok : (i + 1) * tok].astype(BF16)
            dkv_ref[c * wide + i, hd:, :] = dv[:, i * tok : (i + 1) * tok].astype(BF16)
        return carry

    lax.fori_loop(0, peers // wide, one_peer, 0, unroll=True)
    dnkv_ref[:hd, :] = jnp.dot(q_t, ds_ref[:, peers * tok :], preferred_element_type=F32) * scale
    dnkv_ref[hd:, :] = jnp.dot(do_t, p_ref[:, peers * tok :], preferred_element_type=F32)


def row_grad_kernel(recv_ref, dnkv_ref, cpre_ref, npre_ref, gain_ref, g_ref):
    rows, hd = cpre_ref.shape
    summed = recv_ref[0].astype(F32)
    for c in range(1, recv_ref.shape[0]):
        summed = summed + recv_ref[c].astype(F32)
    for copy, (grad_t, pre_ref) in enumerate(((summed, cpre_ref), (dnkv_ref[...], npre_ref))):
        at = slice(copy * rows, (copy + 1) * rows)
        pre = pre_ref[...]
        inverse = lax.rsqrt(jnp.mean(pre * pre, axis=1, keepdims=True) + EPSILON)
        scaled = grad_t[:hd].T * gain_ref[...]
        inner = jnp.mean(scaled * pre, axis=1, keepdims=True)
        pre_grad = inverse * scaled - pre * inverse * inverse * inverse * inner
        g_ref[at, :hd] = pre_grad.astype(BF16)
        g_ref[at, hd:] = grad_t[hd:].T.astype(BF16)


def weight_kernel(mine_ref, theirs_ref, g_ref, their_g_ref, dw_ref):
    dw_ref[...] = (
        jnp.dot(mine_ref[...], g_ref[...], preferred_element_type=F32)
        + jnp.dot(theirs_ref[...], their_g_ref[...], preferred_element_type=F32)
    ).astype(BF16)


def whole(*shape):
    return pl.BlockSpec(shape, lambda *_: (0,) * len(shape))


def left(array):
    return pltpu.with_memory_space_constraint(array, pltpu.HBM)


def limit(mib):
    return pltpu.CompilerParams(vmem_limit_bytes=mib * MIB)


def per_device(
    clean_hidden, noisy_hidden, noisy_query, out_grad, kv_weight, key_gain,
    doc_lengths, clean_place, noisy_place,
):
    rows, width = clean_hidden.shape[1:]
    hd = key_gain.shape[0]
    cp = ("y", "x")
    peers, zs = lax.axis_size(cp), lax.axis_size("z")
    total = clean_place.shape[1] * BLK + rows
    heads = noisy_query.shape[2] // hd
    clean, noisy = clean_hidden[0], noisy_hidden[0]
    gain = key_gain.reshape(1, hd)
    cp_index = lax.axis_index(cp).reshape(1, 1).astype(jnp.int32)
    core_index = lax.axis_index("core").reshape(1, 1).astype(jnp.int32)
    smem = pl.BlockSpec(memory_space=pltpu.SMEM)
    shape = jax.ShapeDtypeStruct
    swap = [(0, 1), (1, 0)]

    parts = 5
    part = width // parts
    anywhere = pl.BlockSpec(memory_space=pl.ANY)
    spread, clean_pre = pl.pallas_call(
        clean_kernel,
        in_specs=[anywhere, anywhere, pl.BlockSpec(memory_space=pltpu.VMEM)],
        out_specs=[anywhere, pl.BlockSpec(memory_space=pltpu.VMEM)],
        out_shape=[shape((peers, rows, 2 * hd), BF16), shape((rows, hd), F32)],
        scratch_shapes=[
            pltpu.VMEM((parts, rows, part), BF16),
            pltpu.VMEM((parts, part, 2 * hd), BF16),
            pltpu.VMEM((rows, 2 * hd), BF16),
            pltpu.SemaphoreType.DMA((parts,)),
            pltpu.SemaphoreType.DMA((parts,)),
            pltpu.SemaphoreType.DMA((peers,)),
        ],
        compiler_params=limit(60),
        cost_estimate=pl.CostEstimate(
            flops=4 * rows * width * hd, bytes_accessed=5 * MIB, transcendentals=0
        ),
        name="clean",
    )(clean, kv_weight, gain)

    spread, clean_later, noisy_later = lax.optimization_barrier((spread, clean, noisy))
    gathered = lax.all_to_all(spread, cp, 0, 0, tiled=True)

    slab = width // zs
    per = slab // (2 * peers)
    turned = shape((peers, per, zs, 2 * rows), BF16)
    nkv, noisy_pre, mask, mine, other = pl.pallas_call(
        prepare_kernel,
        grid=(zs,),
        in_specs=[smem] * 5
        + [pl.BlockSpec((rows, slab), lambda s: (0, s))] * 2
        + [pl.BlockSpec((slab, 2 * hd), lambda s: (s, 0)), whole(1, hd)],
        out_specs=[
            whole(rows, 2 * hd),
            whole(rows, hd),
            whole(total, hd),
            whole(*turned.shape),
            whole(*turned.shape),
        ],
        out_shape=[
            shape((rows, 2 * hd), BF16),
            shape((rows, hd), F32),
            shape((total, hd), BF16),
            turned,
            turned,
        ],
        scratch_shapes=[
            pltpu.VMEM((rows, 2 * hd), F32),
            pltpu.VMEM((2, 2, width // 2, 128), F32),
        ],
        compiler_params=limit(60),
        cost_estimate=pl.CostEstimate(
            flops=4 * rows * width * hd, bytes_accessed=12 * MIB, transcendentals=0
        ),
        name="prepare",
    )(
        cp_index, core_index, doc_lengths, clean_place, noisy_place,
        clean_later, noisy_later, kv_weight, gain,
    )
    theirs = lax.ppermute(other, "core", swap)

    attention, query_grad, dkv, dnkv = pl.pallas_call(
        attention_kernel,
        out_shape=[
            shape((rows, heads * hd), BF16),
            shape((rows, heads * hd), BF16),
            shape((peers, 2 * hd, rows), BF16),
            shape((2 * hd, rows), F32),
        ],
        scratch_shapes=[
            pltpu.VMEM((total, 2 * hd), BF16),
            pltpu.VMEM((total, 2 * hd), BF16),
            pltpu.VMEM((heads * rows, 2 * hd), BF16),
            pltpu.VMEM((heads * rows, 2 * hd), BF16),
            pltpu.VMEM((heads * rows, total), BF16),
            pltpu.VMEM((heads * rows, total), BF16),
        ],
        compiler_params=limit(36),
        cost_estimate=pl.CostEstimate(
            flops=12 * heads * rows * total * hd,
            bytes_accessed=4 * MIB,
            transcendentals=heads * rows * total,
        ),
        name="attend",
    )(
        left(noisy_query[0]), left(out_grad[0]), gathered, left(nkv), left(mask)
    )

    received = lax.all_to_all(dkv, cp, 0, 0, tiled=True)

    row_grad = pl.pallas_call(
        row_grad_kernel,
        out_shape=shape((2 * rows, 2 * hd), BF16),
        compiler_params=limit(8),
        name="row_grad",
    )(received, dnkv, clean_pre, noisy_pre, gain)
    their_grad = lax.ppermute(row_grad, "core", swap)

    columns = width // 2
    tile = columns // 4
    flat = (columns, 2 * rows)
    both = pl.pallas_call(
        weight_kernel,
        grid=(columns // tile,),
        in_specs=[pl.BlockSpec((tile, 2 * rows), lambda s: (s, 0))] * 2
        + [whole(2 * rows, 2 * hd)] * 2,
        out_specs=pl.BlockSpec((tile, 2 * hd), lambda s: (s, 0)),
        out_shape=shape((columns, 2 * hd), BF16),
        compiler_params=limit(8),
        name="weight",
    )(mine.reshape(flat), theirs.reshape(flat), row_grad, their_grad)

    both = lax.all_to_all(both.reshape(peers, per, zs, 2 * hd), cp, 0, 0, tiled=True)
    term = jnp.sum(both.astype(F32), axis=0).astype(BF16)
    term = lax.all_to_all(jnp.swapaxes(term, 0, 1), "z", 0, 0, tiled=True)
    share = jnp.sum(term.astype(F32), axis=0).astype(BF16)
    return (attention[None], query_grad[None], share)


def solution(mesh):
    zs, cps = mesh.devices.shape[0] // 2, mesh.devices.shape[1]
    side = int(round(cps**0.5))
    grid = Mesh(mesh.devices.reshape(zs, 2, cps // side, side), ("z", "core", "y", "x"))
    grp, cp = ("z", "core"), ("y", "x")
    in_specs = (
        P(grp, cp, None),
        P(grp, cp, None),
        P(grp, cp, None),
        P(grp, cp, None),
        P(),
        P(),
        P(grp, None),
        P(grp, None),
        P(grp, None),
    )
    out_specs = (P(grp, cp, None), P(grp, cp, None), P(grp + cp, None))
    return jax.shard_map(
        per_device, mesh=grid, in_specs=in_specs, out_specs=out_specs, check_vma=False
    )
```

```python
import jax
import jax.numpy as jnp
from jax import lax
from jax.experimental import pallas as pl
from jax.experimental.pallas import tpu as pltpu
from jax.sharding import Mesh
from jax.sharding import PartitionSpec as P

BLK = 64
EPSILON = 1e-06
NEGATIVE = -1e30
MIB = 1024 * 1024
LOG2E = 1.4426950408889634

F32 = jnp.float32
BF16 = jnp.bfloat16


def keys_values(joined, gain):
    hd = gain.shape[1]
    pre = joined[:, :hd]
    inverse = lax.rsqrt(jnp.mean(pre * pre, axis=1, keepdims=True) + EPSILON)
    return pre, (pre * inverse * gain).astype(BF16), joined[:, hd:].astype(BF16)


def accumulate(acc_ref, part):
    step = pl.program_id(0)

    @pl.when(step == 0)
    def _():
        acc_ref[...] = part

    @pl.when(step > 0)
    def _():
        acc_ref[...] += part


def clean_kernel(
    clean_ref, w_ref, gain_ref, spread_ref, pre_ref,
    rows_ref, weight_ref, kv_ref, rows_sem, weight_sem, out_sem,
):
    hd = gain_ref.shape[1]
    parts = rows_ref.shape[0]
    part = rows_ref.shape[2]
    loads = []
    for i in range(parts):
        at = pl.ds(i * part, part)
        loads.append(
            (
                pltpu.make_async_copy(w_ref.at[at, :], weight_ref.at[i], weight_sem.at[i]),
                pltpu.make_async_copy(clean_ref.at[:, at], rows_ref.at[i], rows_sem.at[i]),
            )
        )
        for load in loads[i]:
            load.start()
    joined = None
    for i in range(parts):
        for load in loads[i]:
            load.wait()
        term = jnp.dot(rows_ref[i], weight_ref[i], preferred_element_type=F32)
        joined = term if joined is None else joined + term
    pre, keys, values = keys_values(joined, gain_ref[...])
    pre_ref[...] = pre
    kv_ref[:, :hd] = keys
    kv_ref[:, hd:] = values
    stores = [
        pltpu.make_async_copy(kv_ref, spread_ref.at[dest], out_sem.at[dest])
        for dest in range(spread_ref.shape[0])
    ]
    for store in stores:
        store.start()
    for store in stores:
        store.wait()


def prepare_kernel(
    cp_ref, core_ref, len_ref, cplace_ref, nplace_ref, clean_ref, noisy_ref, w_ref, gain_ref,
    nkv_ref, pre_ref, mask_ref, mine_ref, other_ref, acc_ref, turned_ref,
):
    step = pl.program_id(0)
    rows, hd = noisy_ref.shape[0], gain_ref.shape[1]
    half = noisy_ref.shape[1] // 2
    peers, per = mine_ref.shape[0], mine_ref.shape[1]
    accumulate(acc_ref, jnp.dot(noisy_ref[...], w_ref[...], preferred_element_type=F32))
    turned = jnp.concatenate([clean_ref[...], noisy_ref[...]], axis=0).T.astype(F32)
    at = pl.ds(pl.multiple_of(step * half, half), half)
    for core in range(2):
        for lane in range(2):
            turned_ref[core, lane, at, :] = turned[
                core * half : (core + 1) * half, lane * 128 : (lane + 1) * 128
            ]

    @pl.when(step == 0)
    def _():
        blocks, docs = cplace_ref.shape[1], len_ref.shape[1]
        locals_ = rows // BLK
        logical, starts = [], []
        for local in range(locals_):
            slot = cp_ref[0, 0] * locals_ + local
            log = jnp.int32(0)
            for b in range(blocks):
                log = log + jnp.where(nplace_ref[0, b] == slot, b, 0)
            end, start = jnp.int32(0), jnp.int32(0)
            for d in range(docs):
                end = end + len_ref[0, d]
                start = jnp.where(end <= log, end, start)
            logical.append(log)
            starts.append(start)
        lane = lax.broadcasted_iota(jnp.int32, (BLK, hd), 1)
        for b in range(blocks):
            tile = jnp.zeros((BLK, hd), F32)
            for local in range(locals_):
                hidden = jnp.where((starts[local] <= b) & (b < logical[local]), 0.0, NEGATIVE)
                tile = jnp.where(lane == local, hidden, tile)
            slot = pl.multiple_of(cplace_ref[0, b] * BLK, BLK)
            mask_ref[pl.ds(slot, BLK), :] = tile.astype(BF16)
        for local in range(locals_):
            tile = jnp.where((lane < locals_) & (lane != local), NEGATIVE, 0.0)
            first = blocks * BLK + local * BLK
            mask_ref[first : first + BLK, :] = tile.astype(BF16)

    @pl.when(step == pl.num_programs(0) - 1)
    def _():
        pre, keys, values = keys_values(acc_ref[...], gain_ref[...])
        pre_ref[...] = pre
        nkv_ref[:, :hd] = keys
        nkv_ref[:, hd:] = values
        core = core_ref[0, 0]

        def one_peer(j, carry):
            for ref, side in ((other_ref, 1 - core), (mine_ref, core)):
                for i in range(per):
                    for lane in range(2):
                        piece = turned_ref[side, lane, pl.ds(j * per + i, 8, stride=half), :]
                        ref[j, i, :, lane * 128 : (lane + 1) * 128] = piece.astype(BF16)
            return carry

        lax.fori_loop(0, peers, one_peer, 0)


def attention_kernel(
    q_ref, do_ref, ckv_ref, nkv_ref, mask_ref,
    out_ref, dq_ref, dkv_ref, dnkv_ref,
    kx_ref, vx_ref, qx_ref, dox_ref, p_ref, ds_ref, mask_sem,
):
    hd = 128
    tok, heads = q_ref.shape[0], q_ref.shape[1] // hd
    scale = hd ** (-0.5)
    peers = ckv_ref.shape[0]
    total = kx_ref.shape[0]
    mask_load = pltpu.make_async_copy(mask_ref, kx_ref.at[:, pl.ds(hd, hd)], mask_sem)
    mask_load.start()
    for c in range(peers):
        kx_ref[c * tok : (c + 1) * tok, :hd] = ckv_ref[c, :, :hd]
        vx_ref[c * tok : (c + 1) * tok, :hd] = ckv_ref[c, :, hd:]
    kx_ref[peers * tok :, :hd] = nkv_ref[:, :hd]
    vx_ref[peers * tok :, :hd] = nkv_ref[:, hd:]
    vx_ref[:, hd:] = jnp.ones((total, hd), BF16)
    lane = lax.broadcasted_iota(jnp.int32, (tok, hd), 1)
    block = lax.broadcasted_iota(jnp.int32, (tok, hd), 0) // BLK
    pick = jnp.where(lane == block, 1.0, 0.0).astype(BF16)
    for h in range(heads):
        at = slice(h * tok, (h + 1) * tok)
        qx_ref[at, :hd] = q_ref[:, h * hd : (h + 1) * hd]
        qx_ref[at, hd:] = pick
    mask_load.wait()

    def transposed(a, b):
        return lax.dot_general(a, b, (((1,), (1,)), ((), ())), preferred_element_type=F32)

    group = 2 * tok

    def weigh(g, carry):
        at = pl.ds(pl.multiple_of(g * group, group), group)
        s = transposed(qx_ref[at, :], kx_ref[...])
        e = jnp.exp2((s - jnp.max(s, axis=1, keepdims=True)) * (scale * LOG2E))
        p_ref[at, :] = e.astype(BF16)
        return carry

    lax.fori_loop(0, heads * tok // group, weigh, 0, unroll=True)
    for h in range(heads):
        at, cols = slice(h * tok, (h + 1) * tok), slice(h * hd, (h + 1) * hd)
        o = jnp.dot(p_ref[at, :], vx_ref[...], preferred_element_type=F32)
        over = 1.0 / o[:, hd:]
        out = (o[:, :hd] * over).astype(BF16)
        out_ref[:, cols] = out
        do = (do_ref[:, cols].astype(F32) * over).astype(BF16)
        delta = jnp.sum(do.astype(F32) * out.astype(F32), axis=1, keepdims=True)
        high = delta.astype(BF16).astype(F32)
        middle = (delta - high).astype(BF16).astype(F32)
        low = delta - high - middle
        parts = jnp.where(lane == 0, -high, jnp.where(lane == 1, -middle, -low))
        dox_ref[at, :hd] = do
        dox_ref[at, hd:] = jnp.where(lane < 3, parts, 0.0).astype(BF16)

    def slope(g, carry):
        at = pl.ds(pl.multiple_of(g * group, group), group)
        dp = transposed(dox_ref[at, :], vx_ref[...])
        ds_ref[at, :] = (p_ref[at, :].astype(F32) * dp).astype(BF16)
        return carry

    lax.fori_loop(0, heads * tok // group, slope, 0, unroll=True)
    for h in range(heads):
        at, cols = slice(h * tok, (h + 1) * tok), slice(h * hd, (h + 1) * hd)
        dq = jnp.dot(ds_ref[at, :], kx_ref[:, :hd], preferred_element_type=F32)
        dq_ref[:, cols] = (dq * scale).astype(BF16)
    q_t = qx_ref[:, :hd].T
    do_t = dox_ref[:, :hd].T
    wide = 4

    def one_peer(c, carry):
        cols = pl.ds(pl.multiple_of(c * wide * tok, wide * tok), wide * tok)
        dk = jnp.dot(q_t, ds_ref[:, cols], preferred_element_type=F32) * scale
        dv = jnp.dot(do_t, p_ref[:, cols], preferred_element_type=F32)
        for i in range(wide):
            dkv_ref[c * wide + i, :hd, :] = dk[:, i * tok : (i + 1) * tok].astype(BF16)
            dkv_ref[c * wide + i, hd:, :] = dv[:, i * tok : (i + 1) * tok].astype(BF16)
        return carry

    lax.fori_loop(0, peers // wide, one_peer, 0, unroll=True)
    dnkv_ref[:hd, :] = jnp.dot(q_t, ds_ref[:, peers * tok :], preferred_element_type=F32) * scale
    dnkv_ref[hd:, :] = jnp.dot(do_t, p_ref[:, peers * tok :], preferred_element_type=F32)


def row_grad_kernel(recv_ref, dnkv_ref, cpre_ref, npre_ref, gain_ref, g_ref):
    rows, hd = cpre_ref.shape
    summed = recv_ref[0].astype(F32)
    for c in range(1, recv_ref.shape[0]):
        summed = summed + recv_ref[c].astype(F32)
    for copy, (grad_t, pre_ref) in enumerate(((summed, cpre_ref), (dnkv_ref[...], npre_ref))):
        at = slice(copy * rows, (copy + 1) * rows)
        pre = pre_ref[...]
        inverse = lax.rsqrt(jnp.mean(pre * pre, axis=1, keepdims=True) + EPSILON)
        scaled = grad_t[:hd].T * gain_ref[...]
        inner = jnp.mean(scaled * pre, axis=1, keepdims=True)
        pre_grad = inverse * scaled - pre * inverse * inverse * inverse * inner
        g_ref[at, :hd] = pre_grad.astype(BF16)
        g_ref[at, hd:] = grad_t[hd:].T.astype(BF16)


def weight_kernel(mine_ref, theirs_ref, g_ref, their_g_ref, dw_ref):
    dw_ref[...] = (
        jnp.dot(mine_ref[...], g_ref[...], preferred_element_type=F32)
        + jnp.dot(theirs_ref[...], their_g_ref[...], preferred_element_type=F32)
    ).astype(BF16)


def whole(*shape):
    return pl.BlockSpec(shape, lambda *_: (0,) * len(shape))


def left(array):
    return pltpu.with_memory_space_constraint(array, pltpu.HBM)


def limit(mib):
    return pltpu.CompilerParams(vmem_limit_bytes=mib * MIB)


def per_device(
    clean_hidden, noisy_hidden, noisy_query, out_grad, kv_weight, key_gain,
    doc_lengths, clean_place, noisy_place,
):
    rows, width = clean_hidden.shape[1:]
    hd = key_gain.shape[0]
    cp = ("y", "x")
    peers, zs = lax.axis_size(cp), lax.axis_size("z")
    total = clean_place.shape[1] * BLK + rows
    heads = noisy_query.shape[2] // hd
    clean, noisy = clean_hidden[0], noisy_hidden[0]
    gain = key_gain.reshape(1, hd)
    cp_index = lax.axis_index(cp).reshape(1, 1).astype(jnp.int32)
    core_index = lax.axis_index("core").reshape(1, 1).astype(jnp.int32)
    smem = pl.BlockSpec(memory_space=pltpu.SMEM)
    shape = jax.ShapeDtypeStruct
    swap = [(0, 1), (1, 0)]

    parts = 5
    part = width // parts
    anywhere = pl.BlockSpec(memory_space=pl.ANY)
    vmem = pl.BlockSpec(memory_space=pltpu.VMEM)
    spread, clean_pre = pl.pallas_call(
        clean_kernel,
        in_specs=[anywhere, anywhere, pl.BlockSpec(memory_space=pltpu.VMEM)],
        out_specs=[anywhere, pl.BlockSpec(memory_space=pltpu.VMEM)],
        out_shape=[shape((peers, rows, 2 * hd), BF16), shape((rows, hd), F32)],
        scratch_shapes=[
            pltpu.VMEM((parts, rows, part), BF16),
            pltpu.VMEM((parts, part, 2 * hd), BF16),
            pltpu.VMEM((rows, 2 * hd), BF16),
            pltpu.SemaphoreType.DMA((parts,)),
            pltpu.SemaphoreType.DMA((parts,)),
            pltpu.SemaphoreType.DMA((peers,)),
        ],
        compiler_params=limit(60),
        cost_estimate=pl.CostEstimate(
            flops=4 * rows * width * hd, bytes_accessed=5 * MIB, transcendentals=0
        ),
        name="clean",
    )(clean, kv_weight, gain)

    spread, clean_later, noisy_later = lax.optimization_barrier((spread, clean, noisy))
    gathered = lax.all_to_all(spread, cp, 0, 0, tiled=True)

    slab = width // zs
    per = slab // (2 * peers)
    turned = shape((peers, per, zs, 2 * rows), BF16)
    nkv, noisy_pre, mask, mine, other = pl.pallas_call(
        prepare_kernel,
        grid=(zs,),
        in_specs=[smem] * 5
        + [pl.BlockSpec((rows, slab), lambda s: (0, s))] * 2
        + [pl.BlockSpec((slab, 2 * hd), lambda s: (s, 0)), whole(1, hd)],
        out_specs=[
            whole(rows, 2 * hd),
            whole(rows, hd),
            whole(total, hd),
            whole(*turned.shape),
            whole(*turned.shape),
        ],
        out_shape=[
            shape((rows, 2 * hd), BF16),
            shape((rows, hd), F32),
            shape((total, hd), BF16),
            turned,
            turned,
        ],
        scratch_shapes=[
            pltpu.VMEM((rows, 2 * hd), F32),
            pltpu.VMEM((2, 2, width // 2, 128), F32),
        ],
        compiler_params=limit(60),
        cost_estimate=pl.CostEstimate(
            flops=4 * rows * width * hd, bytes_accessed=12 * MIB, transcendentals=0
        ),
        name="prepare",
    )(
        cp_index, core_index, doc_lengths, clean_place, noisy_place,
        clean_later, noisy_later, kv_weight, gain,
    )
    theirs = lax.ppermute(other, "core", swap)

    attention, query_grad, dkv, dnkv = pl.pallas_call(
        attention_kernel,
        in_specs=[vmem] * 4 + [anywhere],
        out_shape=[
            shape((rows, heads * hd), BF16),
            shape((rows, heads * hd), BF16),
            shape((peers, 2 * hd, rows), BF16),
            shape((2 * hd, rows), F32),
        ],
        scratch_shapes=[
            pltpu.VMEM((total, 2 * hd), BF16),
            pltpu.VMEM((total, 2 * hd), BF16),
            pltpu.VMEM((heads * rows, 2 * hd), BF16),
            pltpu.VMEM((heads * rows, 2 * hd), BF16),
            pltpu.VMEM((heads * rows, total), BF16),
            pltpu.VMEM((heads * rows, total), BF16),
            pltpu.SemaphoreType.DMA,
        ],
        compiler_params=limit(36),
        cost_estimate=pl.CostEstimate(
            flops=12 * heads * rows * total * hd,
            bytes_accessed=4 * MIB,
            transcendentals=heads * rows * total,
        ),
        name="attend",
    )(
        left(noisy_query[0]), left(out_grad[0]), gathered, left(nkv), left(mask)
    )

    received = lax.all_to_all(dkv, cp, 0, 0, tiled=True)

    row_grad = pl.pallas_call(
        row_grad_kernel,
        out_shape=shape((2 * rows, 2 * hd), BF16),
        compiler_params=limit(8),
        name="row_grad",
    )(received, dnkv, clean_pre, noisy_pre, gain)
    their_grad = lax.ppermute(row_grad, "core", swap)

    columns = width // 2
    tile = columns // 4
    flat = (columns, 2 * rows)
    both = pl.pallas_call(
        weight_kernel,
        grid=(columns // tile,),
        in_specs=[pl.BlockSpec((tile, 2 * rows), lambda s: (s, 0))] * 2
        + [whole(2 * rows, 2 * hd)] * 2,
        out_specs=pl.BlockSpec((tile, 2 * hd), lambda s: (s, 0)),
        out_shape=shape((columns, 2 * hd), BF16),
        compiler_params=limit(8),
        name="weight",
    )(mine.reshape(flat), theirs.reshape(flat), row_grad, their_grad)

    both = lax.all_to_all(both.reshape(peers, per, zs, 2 * hd), cp, 0, 0, tiled=True)
    term = jnp.sum(both.astype(F32), axis=0).astype(BF16)
    term = lax.all_to_all(jnp.swapaxes(term, 0, 1), "z", 0, 0, tiled=True)
    share = jnp.sum(term.astype(F32), axis=0).astype(BF16)
    return (attention[None], query_grad[None], share)


def solution(mesh):
    zs, cps = mesh.devices.shape[0] // 2, mesh.devices.shape[1]
    side = int(round(cps**0.5))
    grid = Mesh(mesh.devices.reshape(zs, 2, cps // side, side), ("z", "core", "y", "x"))
    grp, cp = ("z", "core"), ("y", "x")
    in_specs = (
        P(grp, cp, None),
        P(grp, cp, None),
        P(grp, cp, None),
        P(grp, cp, None),
        P(),
        P(),
        P(grp, None),
        P(grp, None),
        P(grp, None),
    )
    out_specs = (P(grp, cp, None), P(grp, cp, None), P(grp + cp, None))
    return jax.shard_map(
        per_device, mesh=grid, in_specs=in_specs, out_specs=out_specs, check_vma=False
    )
```
